32 devices in a mesh: row: 4 (over y, x), col: 8 (over z, core).
Axes of the slice: x: 2, y: 2, z: 4, core: 2. Of those that a mesh axis runs over, the one named last changes fastest.
Arguments:
- adjoint: bfloat16 [64, 16384], P(None, ('row', 'col')), may hold values from -6 to 6
- panel_order: int32 [4, 4096], P('row'), may hold values from 0 to 4095, each once within a row
- left_factor: bfloat16 [64, 64, 16, 256], P('row', 'col'), may hold values from -0.375 to 0.375
- right_factor: bfloat16 [64, 64, 16, 256], P('row', 'col'), may hold values from -0.1875 to 0.1875
- tile_ranks: int32 [64, 64], P('row', 'col'), may hold values from 1 to 16
- near_blocks: bfloat16 [4, 8, 8, 256, 256], P('row', 'col'), may hold values from -0.1875 to 0.1875
- near_index: int32 [4, 8, 2, 8], P('row', 'col'), may hold values from 0 to 15, as said below
- near_count: int32 [4, 8], P('row', 'col'), may hold values from 1 to 8, as said below
Outputs:
- result: float32 [64, 16384], P(None, ('col', 'row'))
The draws below stay inside these ranges and needn't reach their ends.
Inputs may be any that keep to these rules, and one draw needn't show every extreme that they name: `near_index`: the 8 slots of one device name distinct tiles of its 16 x 8 block. `near_count`: some device uses all 8 slots.
All inputs are finite; a program needn't handle non-finite values.
Results may differ from the reference program's by a relative error of at most 0.0017.
Values may be sent and summed in bfloat16 or wider, within the bound.
No kernel may reach another device: no remote copies, remote signals or barrier semaphores. Data moves between devices by JAX's collectives and lax.ppermute only.
A program may use at most 64 MiB of HBM per device.

```python
import jax
import jax.numpy as jnp
from jax import lax

K = 64
B = 256
RMAX = 16
RT = 16
CT = 8
NEAR_CAP = 8
TR = 64
TC = 64
NR = 16384
N_ROW = 4
N_COL = 8


def draw_near_index(key, part):
    keys = jax.random.split(jax.random.fold_in(key, 11), N_ROW * N_COL)

    def one_device(device_key):
        chosen = jax.random.permutation(device_key, RT * CT)[:NEAR_CAP].astype(jnp.int32)
        return jnp.stack([chosen // CT, chosen % CT], axis=0)
    return jax.vmap(one_device)(keys).reshape(N_ROW, N_COL, 2, NEAR_CAP).astype(jnp.int32)


def draw_near_count(key, part):
    first_key, second_key, third_key = jax.random.split(jax.random.fold_in(key, 23), 3)
    first = jax.random.randint(first_key, (N_ROW * N_COL,), 0, NEAR_CAP)
    second = jax.random.randint(second_key, (N_ROW * N_COL,), 0, NEAR_CAP)
    counts = 1 + first * second // NEAR_CAP
    chosen = jax.random.randint(third_key, (), 0, N_ROW * N_COL)
    counts = jnp.where(jnp.arange(N_ROW * N_COL) == chosen, NEAR_CAP, counts)
    return counts.reshape(N_ROW, N_COL).astype(jnp.int32)


def with_ends(entries, rng, least, largest):
    extent = entries.shape
    index_at = [jax.random.randint(jax.random.fold_in(rng, axis), (), 0, extent[axis]) for axis in range(len(extent))]
    entries = entries.at[tuple(index_at)].set(least)
    longest = extent.index(max(extent))
    index_at[longest] = (index_at[longest] + 1) % extent[longest]
    return entries.at[tuple(index_at)].set(largest)


def level_of(key, dims, cuts, low, top_value):
    def one(position, shards_of):
        heights = jax.random.uniform(jax.random.fold_in(jax.random.fold_in(key, 6), position), (shards_of,), jnp.float32, low / len(cuts), top_value / len(cuts))
        return jnp.repeat(jnp.exp(heights), dims[position] // shards_of).reshape((-1,) + (1,) * (len(dims) - position - 1))

    level = one(*cuts[0])
    for cut in cuts[1:]:
        level = level * one(*cut)
    return level


def normal_values(rng, extent, spread, most, cuts=(), held_as=jnp.bfloat16):
    entries = jax.random.normal(rng, extent, jnp.float32) * spread
    if len(cuts) > 0:
        entries = level_of(rng, extent, cuts, -0.22, 0.18) * entries
    return jnp.clip(entries, min=-most, max=most).astype(held_as)


def setup_inputs(seed: int = 0) -> dict:
    arg_keys = jax.random.split(jax.random.key(seed), 9)
    adjoint = normal_values(arg_keys[0], (K, NR), 1.0, 6.0, ((1, 32),))
    panel_order = jax.vmap(lambda own: jax.random.permutation(own, RT * B))(jax.random.split(arg_keys[1], N_ROW)).reshape((N_ROW, RT * B)).astype(jnp.int32)
    left_factor = normal_values(arg_keys[2], (TR, TC, RMAX, B), B ** -0.5, 0.375, ((0, 4), (1, 8)))
    right_factor = normal_values(arg_keys[3], (TR, TC, RMAX, B), (TR * RMAX) ** -0.5, 0.1875, ((0, 4), (1, 8)))
    tile_ranks = with_ends(jax.random.randint(arg_keys[4], (TR, TC), 1, RMAX + 1), jax.random.fold_in(arg_keys[4], 1), 1, RMAX).astype(jnp.int32)
    near_blocks = normal_values(arg_keys[5], (N_ROW, N_COL, NEAR_CAP, B, B), (4 * B) ** -0.5, 0.1875, ((0, 4), (1, 8)))
    near_index = draw_near_index(jax.random.fold_in(arg_keys[8], 71), 0)
    near_count = draw_near_count(jax.random.fold_in(arg_keys[8], 71), 0)
    return {"adjoint": adjoint, "panel_order": panel_order, "left_factor": left_factor, "right_factor": right_factor, "tile_ranks": tile_ranks, "near_blocks": near_blocks, "near_index": near_index, "near_count": near_count}


def reference(adjoint, panel_order, left_factor, right_factor, tile_ranks, near_blocks, near_index, near_count):
    group_cols = RT * B
    grouped = adjoint.reshape(K, N_ROW, group_cols)
    rank_range = jnp.arange(RMAX, dtype=jnp.int32)
    slot_range = jnp.arange(NEAR_CAP, dtype=jnp.int32)
    tile_range = jnp.arange(CT, dtype=jnp.int32)

    def one_group(carry, group):
        source = lax.dynamic_index_in_dim(grouped, group, 1, keepdims=False)
        order_row = lax.dynamic_index_in_dim(panel_order, group, 0, keepdims=False)
        tiled = jnp.take(source, order_row, axis=1).reshape(K, RT, B)
        left_part = lax.dynamic_slice_in_dim(left_factor, group * RT, RT, 0)
        right_part = lax.dynamic_slice_in_dim(right_factor, group * RT, RT, 0)
        rank_part = lax.dynamic_slice_in_dim(tile_ranks, group * RT, RT, 0)
        projected = jnp.einsum("kab,acrb->ackr", tiled.astype(jnp.float32), left_part.astype(jnp.float32), precision=lax.Precision.HIGHEST)
        keep = (rank_range[None, None, :] < rank_part[:, :, None])[:, :, None, :]
        projected = jnp.where(keep, projected, 0.0).astype(jnp.bfloat16)
        far_part = jnp.einsum("ackr,acrb->kcb", projected.astype(jnp.float32), right_part.astype(jnp.float32), precision=lax.Precision.HIGHEST)
        blocks = lax.dynamic_index_in_dim(near_blocks, group, 0, keepdims=False)
        index_part = lax.dynamic_index_in_dim(near_index, group, 0, keepdims=False)
        count_part = lax.dynamic_index_in_dim(near_count, group, 0, keepdims=False)
        picked = tiled[:, index_part[:, 0, :], :]
        product = jnp.einsum("kjnb,jnbc->kjnc", picked.astype(jnp.float32), blocks.astype(jnp.float32), precision=lax.Precision.HIGHEST)
        valid = slot_range[None, :] < count_part[:, None]
        product = jnp.where(valid[None, :, :, None], product, 0.0)
        onehot = (index_part[:, 1, :, None] == tile_range[None, None, :]).astype(jnp.float32)
        near_part = jnp.einsum("kjnc,jnt->kjtc", product, onehot, precision=lax.Precision.HIGHEST).reshape(K, N_COL * CT, B)
        return carry + far_part + near_part, None

    total, _ = lax.scan(one_group, jnp.zeros((K, N_COL * CT, B), jnp.float32), jnp.arange(N_ROW, dtype=jnp.int32))
    return total.reshape(K, N_COL * CT * B)
```

```python
import functools

import jax
import jax.numpy as jnp
from jax import lax
from jax.experimental import pallas as pl
from jax.experimental.pallas import tpu as pltpu
from jax.sharding import PartitionSpec as P

F32 = jnp.float32
BF16 = jnp.bfloat16
VMEM = pl.BlockSpec(memory_space=pltpu.VMEM)
SMEM = pl.BlockSpec(memory_space=pltpu.SMEM)


def reorder_tile(tile, ids_ref, first_id, order_ref, units_ref, start):
    width = order_ref.shape[2]
    rows = start.shape[0]
    order = order_ref[tile]
    low = jnp.bitwise_and(order, width - 1)
    high = jnp.right_shift(order, width.bit_length() - 1)
    onehot = jnp.where(lax.broadcasted_iota(jnp.int32, (width, width), 0) == low, 1.0, 0.0).astype(BF16)
    total = start
    slots = units_ref.shape[0] // rows
    for half in range(units_ref.shape[1] // width):
        picked = jnp.dot(units_ref[:, half * width : (half + 1) * width], onehot, preferred_element_type=F32)
        for slot in range(slots):
            own = ids_ref[first_id + half * slots + slot]
            total = jnp.where(high == own, picked[slot * rows : (slot + 1) * rows], total)
    return total


def reorder_kernel(ids_ref, order_ref, units_ref, out_ref):
    tiles, rows, width = out_ref.shape

    def one(tile, carry):
        out_ref[tile] = reorder_tile(tile, ids_ref, 0, order_ref, units_ref, jnp.zeros((rows, width), F32)).astype(BF16)
        return carry

    lax.fori_loop(0, tiles, one, 0, unroll=2)


def main_kernel(
    first_id, ids_ref, rank_ref, index_ref, count_ref, order_ref, units_ref, part_ref, left_ref, right_ref, near_ref,
    out_ref, *refs
):
    *send_refs, x_ref, wide_ref, sum_ref = refs
    tiles, rows, width = x_ref.shape
    _, cols, rank_most, _ = left_ref.shape
    lanes = cols * rank_most

    def one(tile, carry):
        x = reorder_tile(tile, ids_ref, first_id, order_ref, units_ref, part_ref[tile].astype(F32)).astype(BF16)
        x_ref[tile] = x
        left = left_ref[tile].reshape(lanes, width)
        projected = lax.dot_general(x, left, (((1,), (1,)), ((), ())), preferred_element_type=F32)
        lane = lax.broadcasted_iota(jnp.int32, (1, lanes), 1)
        for col in range(cols):
            keep = (lane >= col * rank_most) & (lane < col * rank_most + rank_ref[tile, col])
            wide_ref[tile, col * rows : (col + 1) * rows, :] = jnp.where(keep, projected, 0.0).astype(BF16)
        return carry

    lax.fori_loop(0, tiles, one, 0, unroll=2)
    wide = jnp.concatenate([wide_ref[tile] for tile in range(tiles)], axis=1)
    right = right_ref[...].reshape(tiles * lanes, width)
    far = jnp.dot(wide, right, preferred_element_type=F32)
    pieces = width // 128
    for col in range(cols):
        for piece in range(pieces):
            sum_ref[col * pieces + piece] = far[col * rows : (col + 1) * rows, piece * 128 : (piece + 1) * 128]
    for slot in range(near_ref.shape[0]):
        product = jnp.dot(x_ref[index_ref[0, slot]], near_ref[slot], preferred_element_type=F32)
        product = jnp.where(slot < count_ref[0], product, 0.0)
        at = index_ref[1, slot] * pieces
        for piece in range(pieces):
            sum_ref[at + piece] += product[:, piece * 128 : (piece + 1) * 128]
    row = count_ref[1]
    blocks = out_ref.shape[1] // 128
    for block in range(blocks):
        out_ref[:, block * 128 : (block + 1) * 128] = sum_ref[row * blocks + block]
    for distance, send_ref in enumerate(send_refs, 1):
        to = jnp.bitwise_xor(row, distance)
        for block in range(blocks):
            send_ref[:, block * 128 : (block + 1) * 128] = sum_ref[to * blocks + block].astype(send_ref.dtype)


def local(sizes, adjoint, panel_order, left, right, tile_ranks, near_blocks, near_index, near_count):
    n_row, n_col = sizes
    rows, own_cols = adjoint.shape
    tiles, cols, rank_most, width = left.shape
    order = panel_order.reshape(tiles, 1, width)
    row, col = lax.axis_index("row"), lax.axis_index("col")
    swap = lambda x, axis, n, d: lax.ppermute(x, axis, [(i, i ^ d) for i in range(n)])
    if own_cols % width == 0:
        slots, halves = n_col // 2, own_cols // width
        mine = jnp.concatenate([adjoint] + [swap(adjoint, "col", n_col, d) for d in range(2, n_col, 2)], 0)
        theirs = swap(mine, "col", n_col, 1)
        near = jnp.arange(slots, dtype=jnp.int32) * 2
        ids = jnp.concatenate(
            [jnp.bitwise_xor(near + core, col) * halves + half for core in range(2) for half in range(halves)]
        ).astype(jnp.int32)
    else:
        slots, halves = 1, tiles // 2
        mine, theirs = jnp.split(lax.all_gather(adjoint, "col", axis=1, tiled=True), 2, axis=1)
        ids = jnp.arange(tiles, dtype=jnp.int32)
    part = pl.pallas_call(
        reorder_kernel,
        out_shape=jax.ShapeDtypeStruct((tiles, rows, width), BF16),
        in_specs=[SMEM, VMEM, VMEM],
        out_specs=VMEM,
        cost_estimate=pl.CostEstimate(flops=rows * tiles * width * width * slots * halves * 2, bytes_accessed=0, transcendentals=0),
        compiler_params=pltpu.CompilerParams(vmem_limit_bytes=16 << 20),
        name="reorder",
    )(ids, order, mine)
    out_cols = cols * width // n_row
    counts = jnp.stack([near_count[0, 0], row.astype(jnp.int32)])
    out, *sends = pl.pallas_call(
        functools.partial(main_kernel, slots * halves),
        out_shape=[jax.ShapeDtypeStruct((rows, out_cols), F32)]
        + [jax.ShapeDtypeStruct((rows, out_cols), BF16)] * (n_row - 1),
        in_specs=[SMEM] * 4 + [VMEM] * 6,
        out_specs=[VMEM] * n_row,
        scratch_shapes=[
            pltpu.VMEM((tiles, rows, width), BF16),
            pltpu.VMEM((tiles, cols * rows, cols * rank_most), BF16),
            pltpu.VMEM((cols * width // 128, rows, 128), F32),
        ],
        compiler_params=pltpu.CompilerParams(vmem_limit_bytes=32 << 20),
        name="apply",
    )(ids, tile_ranks, near_index[0, 0], counts, order, theirs, part, left, right, near_blocks[0, 0])
    for distance, send in enumerate(sends, 1):
        out = out + swap(send, "row", n_row, distance).astype(F32)
    return out


def solution(mesh):
    placed = (
        P(None, ("row", "col")),
        P("row", None),
        P("row", "col", None, None),
        P("row", "col", None, None),
        P("row", "col"),
        P("row", "col", None, None, None),
        P("row", "col", None, None),
        P("row", "col"),
    )
    sizes = (mesh.shape["row"], mesh.shape["col"])
    return jax.shard_map(
        functools.partial(local, sizes), mesh=mesh, in_specs=placed, out_specs=P(None, ("col", "row")), check_vma=False
    )
```

```python
import functools

import jax
import jax.numpy as jnp
from jax import lax
from jax.experimental import pallas as pl
from jax.experimental.pallas import tpu as pltpu
from jax.sharding import PartitionSpec as P

F32 = jnp.float32
BF16 = jnp.bfloat16
VMEM = pl.BlockSpec(memory_space=pltpu.VMEM)
SMEM = pl.BlockSpec(memory_space=pltpu.SMEM)
ROW, COL, COUNT, INDEX = 0, 1, 2, 3


def slab_blocks(meta_ref, slabs, width):
    blocks = []
    for ref, distances in slabs:
        halves = ref.shape[1] // width
        for half in range(halves):
            ids = [half if d is None else jnp.bitwise_xor(meta_ref[COL], d) * halves + half for d in distances]
            blocks.append((ref, half, ids))
    return blocks


def reorder_tile(tile, order_ref, blocks, total):
    rows, width = total.shape
    order = order_ref[tile]
    low = jnp.bitwise_and(order, width - 1)
    high = jnp.right_shift(order, width.bit_length() - 1)
    onehot = jnp.where(lax.broadcasted_iota(jnp.int32, (width, width), 0) == low, 1.0, 0.0).astype(BF16)
    for ref, half, ids in blocks:
        picked = jnp.dot(ref[:, half * width : (half + 1) * width], onehot, preferred_element_type=F32)
        for slot, own in enumerate(ids):
            total = jnp.where(high == own, picked[slot * rows : (slot + 1) * rows], total)
    return total


def reorder_kernel(distances, first, meta_ref, order_ref, *refs):
    out_ref = refs[len(distances) + (not first)]
    for spare_ref in refs[len(distances) + (not first) + 1 :]:
        spare_ref[...] = jnp.zeros(spare_ref.shape, spare_ref.dtype)
    slabs = list(zip(refs, distances))
    tiles, rows, width = out_ref.shape
    blocks = slab_blocks(meta_ref, slabs, width)
    for tile in range(tiles):
        total = jnp.zeros((rows, width), F32) if first else refs[len(distances)][tile].astype(F32)
        out_ref[tile] = reorder_tile(tile, order_ref, blocks, total).astype(BF16)


def main_kernel(distances, meta_ref, order_ref, left_ref, right_ref, near_ref, part_ref, *refs):
    slabs = list(zip(refs, distances))
    out_ref, *send_refs, x_ref, wide_ref, sum_ref = refs[len(distances) :]
    tiles, rows, width = x_ref.shape
    _, cols, rank_most, _ = left_ref.shape
    slot_most = near_ref.shape[0]
    lanes = cols * rank_most
    blocks = slab_blocks(meta_ref, slabs, width)
    lane = lax.broadcasted_iota(jnp.int32, (1, lanes), 1)
    for tile in range(tiles):
        x = reorder_tile(tile, order_ref, blocks, part_ref[tile].astype(F32)).astype(BF16)
        x_ref[tile] = x
        left = left_ref[tile].reshape(lanes, width)
        projected = lax.dot_general(x, left, (((1,), (1,)), ((), ())), preferred_element_type=F32)
        for col in range(cols):
            rank = meta_ref[INDEX + 2 * slot_most + tile * cols + col]
            keep = (lane >= col * rank_most) & (lane < col * rank_most + rank)
            wide_ref[tile, col * rows : (col + 1) * rows, :] = jnp.where(keep, projected, 0.0).astype(BF16)
    wide = jnp.concatenate([wide_ref[tile] for tile in range(tiles)], axis=1)
    right = right_ref[...].reshape(tiles * lanes, width)
    far = jnp.dot(wide, right, preferred_element_type=F32)
    pieces = width // 128
    for col in range(cols):
        for piece in range(pieces):
            sum_ref[col * pieces + piece] = far[col * rows : (col + 1) * rows, piece * 128 : (piece + 1) * 128]
    for slot in range(slot_most):
        product = jnp.dot(x_ref[meta_ref[INDEX + slot]], near_ref[slot], preferred_element_type=F32)
        product = jnp.where(slot < meta_ref[COUNT], product, 0.0)
        at = meta_ref[INDEX + slot_most + slot] * pieces
        for piece in range(pieces):
            sum_ref[at + piece] += product[:, piece * 128 : (piece + 1) * 128]
    row = meta_ref[ROW]
    parts = out_ref.shape[1] // 128
    for part in range(parts):
        out_ref[:, part * 128 : (part + 1) * 128] = sum_ref[row * parts + part]
    for distance, send_ref in enumerate(send_refs, 1):
        to = jnp.bitwise_xor(row, distance)
        for part in range(parts):
            send_ref[:, part * 128 : (part + 1) * 128] = sum_ref[to * parts + part].astype(send_ref.dtype)


def local(sizes, adjoint, panel_order, left, right, tile_ranks, near_blocks, near_index, near_count):
    n_row, n_col = sizes
    rows, own_cols = adjoint.shape
    tiles, cols, rank_most, width = left.shape
    order = panel_order.reshape(tiles, 1, width)
    swap = lambda x, axis, n, d: lax.ppermute(x, axis, [(i, i ^ d) for i in range(n)])
    place = jnp.stack([lax.axis_index("row"), lax.axis_index("col"), near_count[0, 0]]).astype(jnp.int32)
    meta = jnp.concatenate([place, near_index.reshape(-1), tile_ranks.reshape(-1)])

    def reorder(slabs, distances, part=None, spare=0):
        slots = sum(slab.shape[0] * slab.shape[1] for slab in slabs)
        return pl.pallas_call(
            functools.partial(reorder_kernel, distances, part is None),
            out_shape=[jax.ShapeDtypeStruct((tiles, rows, width), BF16)]
            + ([jax.ShapeDtypeStruct((spare, own_cols), BF16)] if spare else []),
            in_specs=[SMEM] + [VMEM] * (1 + len(slabs) + (part is not None)),
            out_specs=[VMEM] * (1 + (spare > 0)),
            cost_estimate=pl.CostEstimate(flops=2 * slots * tiles * width, bytes_accessed=0, transcendentals=0),
            compiler_params=pltpu.CompilerParams(vmem_limit_bytes=16 << 20),
            name="reorder",
        )(meta, order, *slabs, *([] if part is None else [part]))

    if own_cols % width == 0:
        far_off = [n_col - 2] + list(range(2, n_col - 2, 2))
        beside = swap(adjoint, "col", n_col, 1)
        near_part, got = reorder([adjoint, beside], [[0], [1]], spare=len(far_off) * rows)
        for at, d in enumerate(far_off):
            got = lax.dynamic_update_slice_in_dim(got, swap(adjoint, "col", n_col, d), at * rows, 0)
        last, last_off = [swap(got, "col", n_col, 1)], [[d ^ 1 for d in far_off]]
        (part,) = reorder([got], [far_off], near_part)
    else:
        part = jnp.zeros((tiles, rows, width), BF16)
        last, last_off = [lax.all_gather(adjoint, "col", axis=1, tiled=True)], [[None]]
    out_cols = cols * width // n_row
    out, *sends = pl.pallas_call(
        functools.partial(main_kernel, last_off),
        out_shape=[jax.ShapeDtypeStruct((rows, out_cols), F32)]
        + [jax.ShapeDtypeStruct((rows, out_cols), BF16)] * (n_row - 1),
        in_specs=[SMEM] + [VMEM] * (5 + len(last)),
        out_specs=[VMEM] * n_row,
        scratch_shapes=[
            pltpu.VMEM((tiles, rows, width), BF16),
            pltpu.VMEM((tiles, cols * rows, cols * rank_most), BF16),
            pltpu.VMEM((cols * width // 128, rows, 128), F32),
        ],
        compiler_params=pltpu.CompilerParams(vmem_limit_bytes=32 << 20),
        name="apply",
    )(meta, order, left, right, near_blocks[0, 0], part, *last)
    for distance, send in enumerate(sends, 1):
        out = out + swap(send, "row", n_row, distance).astype(F32)
    return out


def solution(mesh):
    placed = (
        P(None, ("row", "col")),
        P("row", None),
        P("row", "col", None, None),
        P("row", "col", None, None),
        P("row", "col"),
        P("row", "col", None, None, None),
        P("row", "col", None, None),
        P("row", "col"),
    )
    sizes = (mesh.shape["row"], mesh.shape["col"])
    return jax.shard_map(
        functools.partial(local, sizes), mesh=mesh, in_specs=placed, out_specs=P(None, ("col", "row")), check_vma=False
    )
```

```python
import functools

import jax
import jax.numpy as jnp
from jax import lax
from jax.experimental import pallas as pl
from jax.experimental.pallas import tpu as pltpu
from jax.sharding import PartitionSpec as P

F32 = jnp.float32
BF16 = jnp.bfloat16
VMEM = pl.BlockSpec(memory_space=pltpu.VMEM)
SMEM = pl.BlockSpec(memory_space=pltpu.SMEM)
ROW, COL, COUNT, INDEX = 0, 1, 2, 3
CODE_BITS = 14.97


def slab_blocks(meta_ref, slabs, width):
    blocks = []
    for ref, distances in slabs:
        halves = ref.shape[1] // width
        for half in range(halves):
            ids = [half if d is None else jnp.bitwise_xor(meta_ref[COL], d) * halves + half for d in distances]
            blocks.append((ref, half, ids))
    return blocks


def reorder_tile(tile, order_ref, blocks, total):
    rows, width = total.shape
    order = order_ref[tile]
    low = jnp.bitwise_and(order, width - 1)
    high = jnp.right_shift(order, width.bit_length() - 1)
    onehot = jnp.where(lax.broadcasted_iota(jnp.int32, (width, width), 0) == low, 1.0, 0.0).astype(BF16)
    if blocks[0][0].shape[0] == rows:
        stacked = jnp.concatenate([ref[:, half * width : (half + 1) * width] for ref, half, _ in blocks], 0)
        blocks = [(stacked, 0, sum([ids for _, _, ids in blocks], []))]
    for ref, half, ids in blocks:
        picked = jnp.dot(ref[:, half * width : (half + 1) * width], onehot, preferred_element_type=F32)
        for slot, own in enumerate(ids):
            total = jnp.where(high == own, picked[slot * rows : (slot + 1) * rows], total)
    return total


def reorder_kernel(distances, first, meta_ref, order_ref, *refs):
    out_ref = refs[len(distances) + (not first)]
    for spare_ref in refs[len(distances) + (not first) + 1 :]:
        spare_ref[...] = jnp.zeros(spare_ref.shape, spare_ref.dtype)
    slabs = list(zip(refs, distances))
    tiles, rows, width = out_ref.shape
    blocks = slab_blocks(meta_ref, slabs, width)
    for tile in range(tiles):
        total = jnp.zeros((rows, width), F32) if first else refs[len(distances)][tile].astype(F32)
        out_ref[tile] = reorder_tile(tile, order_ref, blocks, total).astype(BF16)


def main_kernel(distances, meta_ref, order_ref, left_ref, right_ref, near_ref, part_ref, *refs):
    slabs = list(zip(refs, distances))
    out_ref, *send_refs, x_ref, wide_ref, sum_ref = refs[len(distances) :]
    tiles, rows, width = x_ref.shape
    _, cols, rank_most, _ = left_ref.shape
    slot_most = near_ref.shape[0]
    lanes = cols * rank_most
    blocks = slab_blocks(meta_ref, slabs, width)
    lane = lax.broadcasted_iota(jnp.int32, (1, lanes), 1)
    for tile in range(tiles):
        x_ref[tile] = reorder_tile(tile, order_ref, blocks, part_ref[tile].astype(F32)).astype(BF16)
    for tile in range(tiles):
        x = x_ref[tile]
        left = left_ref[tile].reshape(lanes, width)
        projected = lax.dot_general(x, left, (((1,), (1,)), ((), ())), preferred_element_type=F32)
        for col in range(cols):
            rank = meta_ref[INDEX + 2 * slot_most + tile * cols + col]
            keep = (lane >= col * rank_most) & (lane < col * rank_most + rank)
            wide_ref[tile, col * rows : (col + 1) * rows, :] = jnp.where(keep, projected, 0.0).astype(BF16)
    wide = jnp.concatenate([wide_ref[tile] for tile in range(tiles)], axis=1)
    right = right_ref[...].reshape(tiles * lanes, width)
    far = jnp.dot(wide, right, preferred_element_type=F32)
    pieces = width // 128
    for col in range(cols):
        for piece in range(pieces):
            sum_ref[col * pieces + piece] = far[col * rows : (col + 1) * rows, piece * 128 : (piece + 1) * 128]
    for slot in range(slot_most):
        product = jnp.dot(x_ref[meta_ref[INDEX + slot]], near_ref[slot], preferred_element_type=F32)
        product = jnp.where(slot < meta_ref[COUNT], product, 0.0)
        at = meta_ref[INDEX + slot_most + slot] * pieces
        for piece in range(pieces):
            sum_ref[at + piece] += product[:, piece * 128 : (piece + 1) * 128]
    row = meta_ref[ROW]
    parts = out_ref.shape[1] // 128
    for part in range(parts):
        out_ref[:, part * 128 : (part + 1) * 128] = sum_ref[row * parts + part]
    for distance, send_ref in enumerate(send_refs, 1):
        to = jnp.bitwise_xor(row, distance)
        block = sum_ref[pl.ds(to * parts, parts)].reshape(parts * rows, 128)
        most = jnp.max(jnp.abs(block), axis=(0, 1), keepdims=True)
        power = jnp.ceil(jnp.log2(jnp.maximum(most, 1e-30)) - CODE_BITS)
        code = jnp.clip(jnp.round(block * jnp.exp2(-power)), -32767.0, 32767.0)
        send_ref[: parts * rows] = code.astype(jnp.int32).astype(jnp.int16)
        send_ref[parts * rows :] = jnp.broadcast_to(power.astype(jnp.int32), (16, 128)).astype(jnp.int16)


def finish_kernel(own_ref, *refs):
    *got_refs, out_ref = refs
    rows = own_ref.shape[0]
    parts = own_ref.shape[1] // 128
    steps = [jnp.exp2(got_ref[parts * rows :].astype(F32)[:1]) for got_ref in got_refs]
    for part in range(parts):
        total = own_ref[:, part * 128 : (part + 1) * 128]
        for got_ref, step in zip(got_refs, steps):
            total = total + got_ref[part * rows : (part + 1) * rows].astype(F32) * step
        out_ref[:, part * 128 : (part + 1) * 128] = total


def local(sizes, adjoint, panel_order, left, right, tile_ranks, near_blocks, near_index, near_count):
    n_row, n_col = sizes
    rows, own_cols = adjoint.shape
    tiles, cols, rank_most, width = left.shape
    order = panel_order.reshape(tiles, 1, width)
    swap = lambda x, axis, n, d: lax.ppermute(x, axis, [(i, i ^ d) for i in range(n)])
    place = jnp.stack([lax.axis_index("row"), lax.axis_index("col"), near_count[0, 0]]).astype(jnp.int32)
    meta = jnp.concatenate([place, near_index.reshape(-1), tile_ranks.reshape(-1)])

    def reorder(slabs, distances, part=None, spare=0):
        slots = sum(slab.shape[0] * slab.shape[1] for slab in slabs)
        return pl.pallas_call(
            functools.partial(reorder_kernel, distances, part is None),
            out_shape=[jax.ShapeDtypeStruct((tiles, rows, width), BF16)]
            + ([jax.ShapeDtypeStruct((spare, own_cols), BF16)] if spare else []),
            in_specs=[SMEM] + [VMEM] * (1 + len(slabs) + (part is not None)),
            out_specs=[VMEM] * (1 + (spare > 0)),
            cost_estimate=pl.CostEstimate(flops=2 * slots * tiles * width, bytes_accessed=0, transcendentals=0),
            compiler_params=pltpu.CompilerParams(vmem_limit_bytes=16 << 20),
            name="reorder",
        )(meta, order, *slabs, *([] if part is None else [part]))

    if own_cols % width == 0:
        far_off = [6, 4, 2]
        beside = swap(adjoint, "col", n_col, 1)
        near_part, got = reorder([adjoint, beside], [[0], [1]], spare=len(far_off) * rows)
        for at, d in enumerate(far_off):
            got = lax.dynamic_update_slice_in_dim(got, swap(adjoint, "col", n_col, d), at * rows, 0)
        last, last_off = [swap(got, "col", n_col, 1)], [[d ^ 1 for d in far_off]]
        (part,) = reorder([got], [far_off], near_part)
    else:
        part = jnp.zeros((tiles, rows, width), BF16)
        last, last_off = [lax.all_gather(adjoint, "col", axis=1, tiled=True)], [[None]]
    out_cols = cols * width // n_row
    out, *sends = pl.pallas_call(
        functools.partial(main_kernel, last_off),
        out_shape=[jax.ShapeDtypeStruct((rows, out_cols), F32)]
        + [jax.ShapeDtypeStruct((rows * out_cols // 128 + 16, 128), jnp.int16)] * (n_row - 1),
        in_specs=[SMEM] + [VMEM] * (5 + len(last)),
        out_specs=[VMEM] * n_row,
        scratch_shapes=[
            pltpu.VMEM((tiles, rows, width), BF16),
            pltpu.VMEM((tiles, cols * rows, cols * rank_most), BF16),
            pltpu.VMEM((cols * width // 128, rows, 128), F32),
        ],
        compiler_params=pltpu.CompilerParams(vmem_limit_bytes=32 << 20),
        name="apply",
    )(meta, order, left, right, near_blocks[0, 0], part, *last)
    got = [swap(sends[d - 1], "row", n_row, d) for d in range(n_row - 1, 0, -1)]
    return pl.pallas_call(
        finish_kernel,
        out_shape=jax.ShapeDtypeStruct((rows, out_cols), F32),
        in_specs=[VMEM] * n_row,
        out_specs=VMEM,
        compiler_params=pltpu.CompilerParams(vmem_limit_bytes=4 << 20),
        name="finish",
    )(out, *got)


def solution(mesh):
    placed = (
        P(None, ("row", "col")),
        P("row", None),
        P("row", "col", None, None),
        P("row", "col", None, None),
        P("row", "col"),
        P("row", "col", None, None, None),
        P("row", "col", None, None),
        P("row", "col"),
    )
    sizes = (mesh.shape["row"], mesh.shape["col"])
    return jax.shard_map(
        functools.partial(local, sizes), mesh=mesh, in_specs=placed, out_specs=P(None, ("col", "row")), check_vma=False
    )
```

```python
import functools

import jax
import jax.numpy as jnp
from jax import lax
from jax.experimental import pallas as pl
from jax.experimental.pallas import tpu as pltpu
from jax.sharding import PartitionSpec as P

F32 = jnp.float32
BF16 = jnp.bfloat16
VMEM = pl.BlockSpec(memory_space=pltpu.VMEM)
ANY = pl.BlockSpec(memory_space=pl.ANY)
ROW, COUNT, INDEX = 0, 1, 2
CODE_BITS = 14.97


def slab_blocks(slabs, width):
    blocks = []
    for ref, distances in slabs:
        halves = ref.shape[1] // width
        blocks += [(ref, half, [distance * halves + half for distance in distances]) for half in range(halves)]
    return blocks


def reorder_tile(tile, order_ref, blocks, total):
    rows, width = total.shape
    order = order_ref[tile]
    low = jnp.bitwise_and(order, width - 1)
    high = jnp.right_shift(order, width.bit_length() - 1)
    onehot = jnp.where(lax.broadcasted_iota(jnp.int32, (width, width), 0) == low, 1.0, 0.0).astype(BF16)
    if blocks[0][0].shape[0] == rows:
        stacked = jnp.concatenate([ref[:, half * width : (half + 1) * width] for ref, half, _ in blocks], 0)
        blocks = [(stacked, 0, sum([ids for _, _, ids in blocks], []))]
    for ref, half, ids in blocks:
        picked = jnp.dot(ref[:, half * width : (half + 1) * width], onehot, preferred_element_type=F32)
        for slot, own in enumerate(ids):
            total = jnp.where(high == own, picked[slot * rows : (slot + 1) * rows], total)
    return total


def reorder_kernel(distances, first, order_ref, *refs):
    out_ref = refs[len(distances) + 1]
    for spare_ref in refs[len(distances) + 2 :]:
        spare_ref[...] = jnp.zeros(spare_ref.shape, spare_ref.dtype)
    slabs = list(zip(refs, distances))
    tiles, rows, width = out_ref.shape
    blocks = slab_blocks(slabs, width)
    for tile in range(tiles):
        total = jnp.zeros((rows, width), F32) if first else refs[len(distances)][tile].astype(F32)
        out_ref[tile] = reorder_tile(tile, order_ref, blocks, total).astype(BF16)


def main_kernel(distances, meta_hbm, order_ref, left_ref, right_ref, near_ref, part_ref, *refs):
    slabs = list(zip(refs, distances))
    out_ref, *send_refs, x_ref, wide_ref, sum_ref, meta_ref, meta_sem = refs[len(distances) :]
    meta_copy = pltpu.make_async_copy(meta_hbm, meta_ref, meta_sem)
    meta_copy.start()
    tiles, rows, width = x_ref.shape
    _, cols, rank_most, _ = left_ref.shape
    slot_most = near_ref.shape[0]
    lanes = cols * rank_most
    blocks = slab_blocks(slabs, width)
    lane = lax.broadcasted_iota(jnp.int32, (1, lanes), 1)
    for tile in range(tiles):
        x_ref[tile] = reorder_tile(tile, order_ref, blocks, part_ref[tile].astype(F32)).astype(BF16)
    meta_copy.wait()
    for tile in range(tiles):
        x = x_ref[tile]
        left = left_ref[tile].reshape(lanes, width)
        projected = lax.dot_general(x, left, (((1,), (1,)), ((), ())), preferred_element_type=F32)
        for col in range(cols):
            rank = meta_ref[INDEX + 2 * slot_most + tile * cols + col]
            keep = (lane >= col * rank_most) & (lane < col * rank_most + rank)
            wide_ref[tile, col * rows : (col + 1) * rows, :] = jnp.where(keep, projected, 0.0).astype(BF16)
    wide = jnp.concatenate([wide_ref[tile] for tile in range(tiles)], axis=1)
    right = right_ref[...].reshape(tiles * lanes, width)
    far = jnp.dot(wide, right, preferred_element_type=F32)
    pieces = width // 128
    for col in range(cols):
        for piece in range(pieces):
            sum_ref[col * pieces + piece] = far[col * rows : (col + 1) * rows, piece * 128 : (piece + 1) * 128]
    for slot in range(slot_most):
        product = jnp.dot(x_ref[meta_ref[INDEX + slot]], near_ref[slot], preferred_element_type=F32)
        product = jnp.where(slot < meta_ref[COUNT], product, 0.0)
        at = meta_ref[INDEX + slot_most + slot] * pieces
        for piece in range(pieces):
            sum_ref[at + piece] += product[:, piece * 128 : (piece + 1) * 128]
    row = meta_ref[ROW]
    parts = out_ref.shape[1] // 128
    for part in range(parts):
        out_ref[:, part * 128 : (part + 1) * 128] = sum_ref[row * parts + part]
    for distance, send_ref in enumerate(send_refs, 1):
        to = jnp.bitwise_xor(row, distance)
        block = sum_ref[pl.ds(to * parts, parts)].reshape(parts * rows, 128)
        most = jnp.max(jnp.abs(block), axis=(0, 1), keepdims=True)
        power = jnp.ceil(jnp.log2(jnp.maximum(most, 1e-30)) - CODE_BITS)
        code = jnp.clip(jnp.round(block * jnp.exp2(-power)), -32767.0, 32767.0)
        send_ref[: parts * rows] = code.astype(jnp.int32).astype(jnp.int16)
        send_ref[parts * rows :] = jnp.broadcast_to(power.astype(jnp.int32), (16, 128)).astype(jnp.int16)


def finish_kernel(own_ref, *refs):
    *got_refs, out_ref = refs
    rows = own_ref.shape[0]
    parts = own_ref.shape[1] // 128
    steps = [jnp.exp2(got_ref[parts * rows :].astype(F32)[:1]) for got_ref in got_refs]
    for part in range(parts):
        total = own_ref[:, part * 128 : (part + 1) * 128]
        for got_ref, step in zip(got_refs, steps):
            total = total + got_ref[part * rows : (part + 1) * rows].astype(F32) * step
        out_ref[:, part * 128 : (part + 1) * 128] = total


def local(sizes, adjoint, panel_order, left, right, tile_ranks, near_blocks, near_index, near_count):
    n_row, n_col = sizes
    rows, own_cols = adjoint.shape
    tiles, cols, rank_most, width = left.shape
    swap = lambda x, axis, n, d: lax.ppermute(x, axis, [(i, i ^ d) for i in range(n)])
    place = jnp.stack([lax.axis_index("row"), near_count[0, 0]]).astype(jnp.int32)
    meta = jnp.concatenate([place, near_index.reshape(-1), tile_ranks.reshape(-1)])
    meta = jnp.pad(meta, (0, -meta.shape[0] % 128))

    def reorder(slabs, distances, part=None, spare=0):
        slots = sum(slab.shape[0] * slab.shape[1] for slab in slabs)
        return pl.pallas_call(
            functools.partial(reorder_kernel, distances, part is None),
            out_shape=[jax.ShapeDtypeStruct((tiles, rows, width), BF16)]
            + ([jax.ShapeDtypeStruct((spare, own_cols), BF16)] if spare else []),
            in_specs=[VMEM] * (1 + len(slabs) + (part is not None)) + [ANY] * (part is None),
            out_specs=[VMEM] * (1 + (spare > 0)),
            cost_estimate=pl.CostEstimate(flops=2 * slots * tiles * width if part is None else 1000, bytes_accessed=0, transcendentals=0),
            compiler_params=pltpu.CompilerParams(vmem_limit_bytes=16 << 20),
            name="reorder",
        )(order, *slabs, meta if part is None else part)

    if own_cols % width == 0 and own_cols & (own_cols - 1) == 0:
        order = jnp.bitwise_xor(panel_order, lax.axis_index("col") * own_cols).reshape(tiles, 1, width)
        far_off = [n_col - 2] + list(range(2, n_col - 2, 2))
        beside = swap(adjoint, "col", n_col, 1)
        near_part, got = reorder([adjoint, beside], [[0], [1]], spare=len(far_off) * rows)
        for at, d in enumerate(far_off):
            got = lax.dynamic_update_slice_in_dim(got, swap(adjoint, "col", n_col, d), at * rows, 0)
        last, last_off = [swap(got, "col", n_col, 1)], [[d ^ 1 for d in far_off]]
        (part,) = reorder([got], [far_off], near_part)
    else:
        order = panel_order.reshape(tiles, 1, width)
        part = jnp.zeros((tiles, rows, width), BF16)
        last, last_off = [lax.all_gather(adjoint, "col", axis=1, tiled=True)], [[0]]
    out_cols = cols * width // n_row
    out, *sends = pl.pallas_call(
        functools.partial(main_kernel, last_off),
        out_shape=[jax.ShapeDtypeStruct((rows, out_cols), F32)]
        + [jax.ShapeDtypeStruct((rows * out_cols // 128 + 16, 128), jnp.int16)] * (n_row - 1),
        in_specs=[ANY] + [VMEM] * (5 + len(last)),
        out_specs=[VMEM] * n_row,
        scratch_shapes=[
            pltpu.VMEM((tiles, rows, width), BF16),
            pltpu.VMEM((tiles, cols * rows, cols * rank_most), BF16),
            pltpu.VMEM((cols * width // 128, rows, 128), F32),
            pltpu.SMEM(meta.shape, jnp.int32),
            pltpu.SemaphoreType.DMA(()),
        ],
        compiler_params=pltpu.CompilerParams(vmem_limit_bytes=32 << 20),
        name="apply",
    )(meta, order, left, right, near_blocks[0, 0], part, *last)
    got = [swap(sends[d - 1], "row", n_row, d) for d in range(n_row - 1, 0, -1)]
    return pl.pallas_call(
        finish_kernel,
        out_shape=jax.ShapeDtypeStruct((rows, out_cols), F32),
        in_specs=[VMEM] * n_row,
        out_specs=VMEM,
        compiler_params=pltpu.CompilerParams(vmem_limit_bytes=4 << 20),
        name="finish",
    )(out, *got)


def solution(mesh):
    placed = (
        P(None, ("row", "col")),
        P("row", None),
        P("row", "col", None, None),
        P("row", "col", None, None),
        P("row", "col"),
        P("row", "col", None, None, None),
        P("row", "col", None, None),
        P("row", "col"),
    )
    sizes = (mesh.shape["row"], mesh.shape["col"])
    return jax.shard_map(
        functools.partial(local, sizes), mesh=mesh, in_specs=placed, out_specs=P(None, ("col", "row")), check_vma=False
    )
```

```python
import functools

import jax
import jax.numpy as jnp
from jax import lax
from jax.experimental import pallas as pl
from jax.experimental.pallas import tpu as pltpu
from jax.sharding import PartitionSpec as P

F32 = jnp.float32
BF16 = jnp.bfloat16
VMEM = pl.BlockSpec(memory_space=pltpu.VMEM)
ANY = pl.BlockSpec(memory_space=pl.ANY)
COUNT, INDEX = 0, 1
CODE_BITS = 14.97


def slab_blocks(slabs, width):
    blocks = []
    for ref, distances in slabs:
        halves = ref.shape[1] // width
        blocks += [(ref, half, [distance * halves + half for distance in distances]) for half in range(halves)]
    return blocks


def reorder_tile(tile, order_ref, blocks, total):
    rows, width = total.shape
    order = order_ref[tile]
    low = jnp.bitwise_and(order, width - 1)
    high = jnp.right_shift(order, width.bit_length() - 1)
    onehot = jnp.where(lax.broadcasted_iota(jnp.int32, (width, width), 0) == low, 1.0, 0.0).astype(BF16)
    if blocks[0][0].shape[0] == rows:
        stacked = jnp.concatenate([ref[:, half * width : (half + 1) * width] for ref, half, _ in blocks], 0)
        blocks = [(stacked, 0, sum([ids for _, _, ids in blocks], []))]
    for ref, half, ids in blocks:
        picked = jnp.dot(ref[:, half * width : (half + 1) * width], onehot, preferred_element_type=F32)
        for slot, own in enumerate(ids):
            total = jnp.where(high == own, picked[slot * rows : (slot + 1) * rows], total)
    return total


def pack_scalars(small, small_refs, sems, packed_ref):
    copies = [pltpu.make_async_copy(a, b, sems.at[at]) for at, (a, b) in enumerate(zip(small, small_refs))]
    for copy in copies:
        copy.start()
    for copy in copies:
        copy.wait()
    at = 0
    for ref in small_refs:
        for i in range(ref.shape[0]):
            for j in range(ref.shape[1]):
                packed_ref[at] = ref[i, j]
                at += 1


def reorder_kernel(distances, first, order_ref, *refs):
    out_ref = refs[len(distances) + (3 if first else 1)]
    if first:
        *refs, s0, s1, s2, sems = refs
        pack_scalars(refs[len(distances) : len(distances) + 3], (s0, s1, s2), sems, refs[-1])
        refs = refs[:-1]
    for spare_ref in refs[len(distances) + (3 if first else 1) + 1 :]:
        spare_ref[...] = jnp.zeros(spare_ref.shape, spare_ref.dtype)
    slabs = list(zip(refs, distances))
    tiles, rows, width = out_ref.shape
    blocks = slab_blocks(slabs, width)
    for tile in range(tiles):
        total = jnp.zeros((rows, width), F32) if first else refs[len(distances)][tile].astype(F32)
        out_ref[tile] = reorder_tile(tile, order_ref, blocks, total).astype(BF16)


def main_kernel(distances, meta_hbm, order_ref, left_ref, right_ref, near_ref, part_ref, *refs):
    slabs = list(zip(refs, distances))
    out_ref, *send_refs, x_ref, wide_ref, sum_ref, meta_ref, meta_sem = refs[len(distances) :]
    meta_copy = pltpu.make_async_copy(meta_hbm, meta_ref, meta_sem)
    meta_copy.start()
    tiles, rows, width = x_ref.shape
    _, cols, rank_most, _ = left_ref.shape
    slot_most = near_ref.shape[0]
    lanes = cols * rank_most
    rank_at = lax.broadcasted_iota(jnp.int32, (rank_most, rows), 0)
    blocks = slab_blocks(slabs, width)
    for tile in range(tiles):
        x_ref[tile] = reorder_tile(tile, order_ref, blocks, part_ref[tile].astype(F32)).astype(BF16)
    meta_copy.wait()
    for tile in range(tiles):
        x = x_ref[tile]
        left = left_ref[tile].reshape(lanes, width)
        projected = lax.dot_general(left, x, (((1,), (1,)), ((), ())), preferred_element_type=F32)
        for col in range(cols):
            keep = rank_at < meta_ref[INDEX + 2 * slot_most + col * tiles + tile]
            kept = jnp.where(keep, projected[col * rank_most : (col + 1) * rank_most], 0.0)
            wide_ref[col, tile * rank_most : (tile + 1) * rank_most, :] = kept.astype(BF16)
    pieces = width // 128
    for col in range(cols):
        right = right_ref[:, col].reshape(tiles * rank_most, width)
        far = lax.dot_general(wide_ref[col], right, (((0,), (0,)), ((), ())), preferred_element_type=F32)
        for piece in range(pieces):
            sum_ref[col * pieces + piece] = far[:, piece * 128 : (piece + 1) * 128]
    for slot in range(slot_most):
        product = jnp.dot(x_ref[meta_ref[INDEX + slot]], near_ref[slot], preferred_element_type=F32)
        product = jnp.where(slot < meta_ref[COUNT], product, 0.0)
        at = meta_ref[INDEX + slot_most + slot] * pieces
        for piece in range(pieces):
            sum_ref[at + piece] += product[:, piece * 128 : (piece + 1) * 128]
    row = lax.axis_index("row")
    parts = out_ref.shape[1] // 128
    for part in range(parts):
        out_ref[:, part * 128 : (part + 1) * 128] = sum_ref[row * parts + part]
    for distance, send_ref in enumerate(send_refs, 1):
        to = jnp.bitwise_xor(row, distance)
        block = sum_ref[pl.ds(to * parts, parts)].reshape(parts * rows, 128)
        most = jnp.max(jnp.abs(block), axis=(0, 1), keepdims=True)
        power = jnp.ceil(jnp.log2(jnp.maximum(most, 1e-30)) - CODE_BITS)
        code = jnp.clip(jnp.round(block * jnp.exp2(-power)), -32767.0, 32767.0)
        send_ref[: parts * rows] = code.astype(jnp.int32).astype(jnp.int16)
        send_ref[parts * rows :] = jnp.broadcast_to(power.astype(jnp.int32), (16, 128)).astype(jnp.int16)


def finish_kernel(own_ref, *refs):
    *got_refs, out_ref = refs
    rows = own_ref.shape[0]
    parts = own_ref.shape[1] // 128
    steps = [jnp.exp2(got_ref[parts * rows :].astype(F32)[:1]) for got_ref in got_refs]
    for part in range(parts):
        total = own_ref[:, part * 128 : (part + 1) * 128]
        for got_ref, step in zip(got_refs, steps):
            total = total + got_ref[part * rows : (part + 1) * rows].astype(F32) * step
        out_ref[:, part * 128 : (part + 1) * 128] = total


def local(sizes, adjoint, panel_order, left, right, tile_ranks, near_blocks, near_index, near_count):
    n_row, n_col = sizes
    rows, own_cols = adjoint.shape
    tiles, cols, rank_most, width = left.shape
    swap = lambda x, axis, n, d: lax.ppermute(x, axis, [(i, i ^ d) for i in range(n)])
    small = [near_count, near_index[0, 0], tile_ranks.T]
    scalars = sum(x.size for x in small)

    def reorder(slabs, distances, part=None, spare=0):
        slots = sum(slab.shape[0] * slab.shape[1] for slab in slabs)
        return pl.pallas_call(
            functools.partial(reorder_kernel, distances, part is None),
            out_shape=[jax.ShapeDtypeStruct((tiles, rows, width), BF16)]
            + ([jax.ShapeDtypeStruct((spare, own_cols), BF16), jax.ShapeDtypeStruct((-(-scalars // 128) * 128,), jnp.int32)] if spare else []),
            in_specs=[VMEM] * (1 + len(slabs) + (part is not None)) + [ANY] * (3 if part is None else 0),
            out_specs=[VMEM, VMEM, pl.BlockSpec(memory_space=pltpu.SMEM)] if spare else [VMEM],
            scratch_shapes=[pltpu.SMEM(x.shape, jnp.int32) for x in small] + [pltpu.SemaphoreType.DMA((3,))] if spare else [],
            cost_estimate=pl.CostEstimate(flops=2 * slots * tiles * width if part is None else 1000, bytes_accessed=0, transcendentals=0),
            compiler_params=pltpu.CompilerParams(vmem_limit_bytes=16 << 20),
            name="reorder",
        )(order, *slabs, *(small if part is None else [part]))

    if own_cols % width == 0 and own_cols & (own_cols - 1) == 0:
        order = jnp.bitwise_xor(panel_order, lax.axis_index("col") * own_cols).reshape(tiles, 1, width)
        far_off = [n_col - 2] + list(range(2, n_col - 2, 2))
        beside = swap(adjoint, "col", n_col, 1)
        near_part, got, meta = reorder([adjoint, beside], [[0], [1]], spare=len(far_off) * rows)
        for at, d in enumerate(far_off):
            got = lax.dynamic_update_slice_in_dim(got, swap(adjoint, "col", n_col, d), at * rows, 0)
        last, last_off = [swap(got, "col", n_col, 1)], [[d ^ 1 for d in far_off]]
        (part,) = reorder([got], [far_off], near_part)
    else:
        order = panel_order.reshape(tiles, 1, width)
        part = jnp.zeros((tiles, rows, width), BF16)
        meta = jnp.concatenate([x.reshape(-1) for x in small])
        meta = jnp.pad(meta, (0, -scalars % 128))
        last, last_off = [lax.all_gather(adjoint, "col", axis=1, tiled=True)], [[0]]
    out_cols = cols * width // n_row
    out, *sends = pl.pallas_call(
        functools.partial(main_kernel, last_off),
        out_shape=[jax.ShapeDtypeStruct((rows, out_cols), F32)]
        + [jax.ShapeDtypeStruct((rows * out_cols // 128 + 16, 128), jnp.int16)] * (n_row - 1),
        in_specs=[ANY] + [VMEM] * (5 + len(last)),
        out_specs=[VMEM] * n_row,
        scratch_shapes=[
            pltpu.VMEM((tiles, rows, width), BF16),
            pltpu.VMEM((cols, tiles * rank_most, rows), BF16),
            pltpu.VMEM((cols * width // 128, rows, 128), F32),
            pltpu.SMEM(meta.shape, jnp.int32),
            pltpu.SemaphoreType.DMA(()),
        ],
        compiler_params=pltpu.CompilerParams(vmem_limit_bytes=32 << 20),
        name="apply",
    )(meta, order, left, right, near_blocks[0, 0], part, *last)
    got = [swap(sends[d - 1], "row", n_row, d) for d in range(n_row - 1, 0, -1)]
    return pl.pallas_call(
        finish_kernel,
        out_shape=jax.ShapeDtypeStruct((rows, out_cols), F32),
        in_specs=[VMEM] * n_row,
        out_specs=VMEM,
        compiler_params=pltpu.CompilerParams(vmem_limit_bytes=4 << 20),
        name="finish",
    )(out, *got)


def solution(mesh):
    placed = (
        P(None, ("row", "col")),
        P("row", None),
        P("row", "col", None, None),
        P("row", "col", None, None),
        P("row", "col"),
        P("row", "col", None, None, None),
        P("row", "col", None, None),
        P("row", "col"),
    )
    sizes = (mesh.shape["row"], mesh.shape["col"])
    return jax.shard_map(
        functools.partial(local, sizes), mesh=mesh, in_specs=placed, out_specs=P(None, ("col", "row")), check_vma=False
    )
```

```python
import functools

import jax
import jax.numpy as jnp
from jax import lax
from jax.experimental import pallas as pl
from jax.experimental.pallas import tpu as pltpu
from jax.sharding import PartitionSpec as P

F32 = jnp.float32
BF16 = jnp.bfloat16
VMEM = pl.BlockSpec(memory_space=pltpu.VMEM)
ANY = pl.BlockSpec(memory_space=pl.ANY)
COUNT, INDEX = 0, 1
CODE_BITS = 14.97


def slab_blocks(slabs, width):
    blocks = []
    for ref, distances in slabs:
        halves = ref.shape[1] // width
        blocks += [(ref, half, [distance * halves + half for distance in distances]) for half in range(halves)]
    return blocks


def reorder_tile(tile, order_ref, blocks, total):
    rows, width = total.shape
    order = order_ref[tile]
    low = jnp.bitwise_and(order, width - 1)
    high = jnp.right_shift(order, width.bit_length() - 1)
    onehot = jnp.where(lax.broadcasted_iota(jnp.int32, (width, width), 0) == low, 1.0, 0.0).astype(BF16)
    if blocks[0][0].shape[0] == rows:
        stacked = jnp.concatenate([ref[:, half * width : (half + 1) * width] for ref, half, _ in blocks], 0)
        blocks = [(stacked, 0, sum([ids for _, _, ids in blocks], []))]
    for ref, half, ids in blocks:
        picked = jnp.dot(ref[:, half * width : (half + 1) * width], onehot, preferred_element_type=F32)
        for slot, own in enumerate(ids):
            total = jnp.where(high == own, picked[slot * rows : (slot + 1) * rows], total)
    return total


def pack_scalars(small, small_refs, sems, packed_ref):
    copies = [pltpu.make_async_copy(a, b, sems.at[at]) for at, (a, b) in enumerate(zip(small, small_refs))]
    for copy in copies:
        copy.start()
    for copy in copies:
        copy.wait()
    at = 0
    for ref in small_refs:
        for i in range(ref.shape[0]):
            for j in range(ref.shape[1]):
                packed_ref[at] = ref[i, j]
                at += 1


def reorder_kernel(distances, first, order_ref, *refs):
    out_ref = refs[len(distances) + (3 if first else 1)]
    if first:
        *refs, s0, s1, s2, sems = refs
        pack_scalars(refs[len(distances) : len(distances) + 3], (s0, s1, s2), sems, refs[-1])
        refs = refs[:-1]
    for spare_ref in refs[len(distances) + (3 if first else 1) + 1 :]:
        spare_ref[...] = jnp.zeros(spare_ref.shape, spare_ref.dtype)
    slabs = list(zip(refs, distances))
    tiles, rows, width = out_ref.shape
    blocks = slab_blocks(slabs, width)
    for tile in range(tiles):
        total = jnp.zeros((rows, width), F32) if first else refs[len(distances)][tile].astype(F32)
        out_ref[tile] = reorder_tile(tile, order_ref, blocks, total).astype(BF16)


def row_step(row, distance, n_row):
    if n_row != 4 or distance == 3:
        return distance
    turn = (row ^ (row >> 1)) & 1
    return 1 + turn if distance == 1 else 2 - turn


def main_kernel(distances, meta_hbm, order_ref, left_ref, right_ref, near_ref, part_ref, *refs):
    slabs = list(zip(refs, distances))
    out_ref, *send_refs, x_ref, wide_ref, sum_ref, meta_ref, meta_sem = refs[len(distances) :]
    meta_copy = pltpu.make_async_copy(meta_hbm, meta_ref, meta_sem)
    meta_copy.start()
    tiles, rows, width = x_ref.shape
    _, cols, rank_most, _ = left_ref.shape
    slot_most = near_ref.shape[0]
    lanes = cols * rank_most
    rank_at = lax.broadcasted_iota(jnp.int32, (rank_most, rows), 0)
    blocks = slab_blocks(slabs, width)
    for tile in range(tiles):
        x_ref[tile] = reorder_tile(tile, order_ref, blocks, part_ref[tile].astype(F32)).astype(BF16)
    meta_copy.wait()
    for tile in range(tiles):
        x = x_ref[tile]
        left = left_ref[tile].reshape(lanes, width)
        projected = lax.dot_general(left, x, (((1,), (1,)), ((), ())), preferred_element_type=F32)
        for col in range(cols):
            keep = rank_at < meta_ref[INDEX + 2 * slot_most + col * tiles + tile]
            kept = jnp.where(keep, projected[col * rank_most : (col + 1) * rank_most], 0.0)
            wide_ref[col, tile * rank_most : (tile + 1) * rank_most, :] = kept.astype(BF16)
    pieces = width // 128
    for col in range(cols):
        right = right_ref[:, col].reshape(tiles * rank_most, width)
        far = lax.dot_general(wide_ref[col], right, (((0,), (0,)), ((), ())), preferred_element_type=F32)
        for piece in range(pieces):
            sum_ref[col * pieces + piece] = far[:, piece * 128 : (piece + 1) * 128]
    for slot in range(slot_most):
        product = jnp.dot(x_ref[meta_ref[INDEX + slot]], near_ref[slot], preferred_element_type=F32)
        product = jnp.where(slot < meta_ref[COUNT], product, 0.0)
        at = meta_ref[INDEX + slot_most + slot] * pieces
        for piece in range(pieces):
            sum_ref[at + piece] += product[:, piece * 128 : (piece + 1) * 128]
    row = lax.axis_index("row")
    parts = out_ref.shape[1] // 128
    for part in range(parts):
        out_ref[:, part * 128 : (part + 1) * 128] = sum_ref[row * parts + part]
    for distance, send_ref in enumerate(send_refs, 1):
        to = jnp.bitwise_xor(row, row_step(row, distance, len(send_refs) + 1))
        block = sum_ref[pl.ds(to * parts, parts)].reshape(parts * rows, 128)
        most = jnp.max(jnp.abs(block), axis=(0, 1), keepdims=True)
        power = jnp.ceil(jnp.log2(jnp.maximum(most, 1e-30)) - CODE_BITS)
        code = jnp.clip(jnp.round(block * jnp.exp2(-power)), -32767.0, 32767.0)
        send_ref[: parts * rows] = code.astype(jnp.int32).astype(jnp.int16)
        send_ref[parts * rows :] = jnp.broadcast_to(power.astype(jnp.int32), (16, 128)).astype(jnp.int16)


def finish_kernel(own_ref, *refs):
    *got_refs, out_ref = refs
    rows = own_ref.shape[0]
    parts = own_ref.shape[1] // 128
    steps = [jnp.exp2(got_ref[parts * rows :].astype(F32)[:1]) for got_ref in got_refs]
    for part in range(parts):
        total = own_ref[:, part * 128 : (part + 1) * 128]
        for got_ref, step in zip(got_refs, steps):
            total = total + got_ref[part * rows : (part + 1) * rows].astype(F32) * step
        out_ref[:, part * 128 : (part + 1) * 128] = total


def local(sizes, adjoint, panel_order, left, right, tile_ranks, near_blocks, near_index, near_count):
    n_row, n_col = sizes
    rows, own_cols = adjoint.shape
    tiles, cols, rank_most, width = left.shape
    swap = lambda x, axis, n, d: lax.ppermute(x, axis, [(i, i ^ d) for i in range(n)])
    small = [near_count, near_index[0, 0], tile_ranks.T]
    scalars = sum(x.size for x in small)

    def reorder(slabs, distances, part=None, spare=0):
        slots = sum(slab.shape[0] * slab.shape[1] for slab in slabs)
        return pl.pallas_call(
            functools.partial(reorder_kernel, distances, part is None),
            out_shape=[jax.ShapeDtypeStruct((tiles, rows, width), BF16)]
            + ([jax.ShapeDtypeStruct((spare, own_cols), BF16), jax.ShapeDtypeStruct((-(-scalars // 128) * 128,), jnp.int32)] if spare else []),
            in_specs=[VMEM] * (1 + len(slabs) + (part is not None)) + [ANY] * (3 if part is None else 0),
            out_specs=[VMEM, VMEM, pl.BlockSpec(memory_space=pltpu.SMEM)] if spare else [VMEM],
            scratch_shapes=[pltpu.SMEM(x.shape, jnp.int32) for x in small] + [pltpu.SemaphoreType.DMA((3,))] if spare else [],
            cost_estimate=pl.CostEstimate(flops=2 * slots * tiles * width if part is None else 1000, bytes_accessed=0, transcendentals=0),
            compiler_params=pltpu.CompilerParams(vmem_limit_bytes=16 << 20),
            name="reorder",
        )(order, *slabs, *(small if part is None else [part]))

    if own_cols % width == 0 and own_cols & (own_cols - 1) == 0:
        order = jnp.bitwise_xor(panel_order, lax.axis_index("col") * own_cols).reshape(tiles, 1, width)
        far_off = [n_col - 2] + list(range(2, n_col - 2, 2))
        beside = swap(adjoint, "col", n_col, 1)
        near_part, got, meta = reorder([adjoint, beside], [[0], [1]], spare=len(far_off) * rows)
        for at, d in enumerate(far_off):
            got = lax.dynamic_update_slice_in_dim(got, swap(adjoint, "col", n_col, d), at * rows, 0)
        last, last_off = [swap(got, "col", n_col, 1)], [[d ^ 1 for d in far_off]]
        (part,) = reorder([got], [far_off], near_part)
    else:
        order = panel_order.reshape(tiles, 1, width)
        part = jnp.zeros((tiles, rows, width), BF16)
        meta = jnp.concatenate([x.reshape(-1) for x in small])
        meta = jnp.pad(meta, (0, -scalars % 128))
        last, last_off = [lax.all_gather(adjoint, "col", axis=1, tiled=True)], [[0]]
    out_cols = cols * width // n_row
    out, *sends = pl.pallas_call(
        functools.partial(main_kernel, last_off),
        out_shape=[jax.ShapeDtypeStruct((rows, out_cols), F32)]
        + [jax.ShapeDtypeStruct((rows * out_cols // 128 + 16, 128), jnp.int16)] * (n_row - 1),
        in_specs=[ANY] + [VMEM] * (5 + len(last)),
        out_specs=[VMEM] * n_row,
        scratch_shapes=[
            pltpu.VMEM((tiles, rows, width), BF16),
            pltpu.VMEM((cols, tiles * rank_most, rows), BF16),
            pltpu.VMEM((cols * width // 128, rows, 128), F32),
            pltpu.SMEM(meta.shape, jnp.int32),
            pltpu.SemaphoreType.DMA(()),
        ],
        compiler_params=pltpu.CompilerParams(vmem_limit_bytes=32 << 20),
        name="apply",
    )(meta, order, left, right, near_blocks[0, 0], part, *last)
    steps = range(n_row - 1, 0, -1)
    got = [lax.ppermute(sends[d - 1], "row", [(i, i ^ row_step(i, d, n_row)) for i in range(n_row)]) for d in steps]
    return pl.pallas_call(
        finish_kernel,
        out_shape=jax.ShapeDtypeStruct((rows, out_cols), F32),
        in_specs=[VMEM] * n_row,
        out_specs=VMEM,
        compiler_params=pltpu.CompilerParams(vmem_limit_bytes=4 << 20),
        name="finish",
    )(out, *got)


def solution(mesh):
    placed = (
        P(None, ("row", "col")),
        P("row", None),
        P("row", "col", None, None),
        P("row", "col", None, None),
        P("row", "col"),
        P("row", "col", None, None, None),
        P("row", "col", None, None),
        P("row", "col"),
    )
    sizes = (mesh.shape["row"], mesh.shape["col"])
    return jax.shard_map(
        functools.partial(local, sizes), mesh=mesh, in_specs=placed, out_specs=P(None, ("col", "row")), check_vma=False
    )
```

```python
import functools

import jax
import jax.numpy as jnp
from jax import lax
from jax.experimental import pallas as pl
from jax.experimental.pallas import tpu as pltpu
from jax.sharding import PartitionSpec as P

F32 = jnp.float32
BF16 = jnp.bfloat16
VMEM = pl.BlockSpec(memory_space=pltpu.VMEM)
ANY = pl.BlockSpec(memory_space=pl.ANY)
COUNT, INDEX = 0, 1
CODE_BITS = 14.97


def slab_blocks(slabs, width):
    blocks = []
    for ref, distances in slabs:
        halves = ref.shape[1] // width
        blocks += [(ref, half, [distance * halves + half for distance in distances]) for half in range(halves)]
    return blocks


def reorder_tile(tile, order_ref, blocks, total):
    rows, width = total.shape
    order = order_ref[tile]
    low = jnp.bitwise_and(order, width - 1)
    high = jnp.right_shift(order, width.bit_length() - 1)
    onehot = jnp.where(lax.broadcasted_iota(jnp.int32, (width, width), 0) == low, 1.0, 0.0).astype(BF16)
    if blocks[0][0].shape[0] == rows:
        stacked = jnp.concatenate([ref[:, half * width : (half + 1) * width] for ref, half, _ in blocks], 0)
        blocks = [(stacked, 0, sum([ids for _, _, ids in blocks], []))]
    for ref, half, ids in blocks:
        picked = jnp.dot(ref[:, half * width : (half + 1) * width], onehot, preferred_element_type=F32)
        for slot, own in enumerate(ids):
            total = jnp.where(high == own, picked[slot * rows : (slot + 1) * rows], total)
    return total


def pack_scalars(small, small_refs, sems, packed_ref):
    copies = [pltpu.make_async_copy(a, b, sems.at[at]) for at, (a, b) in enumerate(zip(small, small_refs))]
    for copy in copies:
        copy.start()
    for copy in copies:
        copy.wait()
    at = 0
    for ref in small_refs:
        for i in range(ref.shape[0]):
            for j in range(ref.shape[1]):
                packed_ref[at] = ref[i, j]
                at += 1


def reorder_kernel(distances, first, order_ref, *refs):
    out_ref = refs[len(distances) + (3 if first else 1)]
    if first:
        *refs, s0, s1, s2, sems = refs
        pack_scalars(refs[len(distances) : len(distances) + 3], (s0, s1, s2), sems, refs[-1])
        refs = refs[:-1]
    for spare_ref in refs[len(distances) + (3 if first else 1) + 1 :]:
        spare_ref[...] = jnp.zeros(spare_ref.shape, spare_ref.dtype)
    slabs = list(zip(refs, distances))
    tiles, rows, width = out_ref.shape
    blocks = slab_blocks(slabs, width)
    for tile in range(tiles):
        total = jnp.zeros((rows, width), F32) if first else refs[len(distances)][tile].astype(F32)
        out_ref[tile] = reorder_tile(tile, order_ref, blocks, total).astype(BF16)


def main_kernel(distances, meta_hbm, order_ref, left_ref, right_ref, near_ref, part_ref, *refs):
    slabs = list(zip(refs, distances))
    out_ref, *send_refs, x_ref, wide_ref, sum_ref, meta_ref, meta_sem = refs[len(distances) :]
    meta_copy = pltpu.make_async_copy(meta_hbm, meta_ref, meta_sem)
    meta_copy.start()
    tiles, rows, width = x_ref.shape
    _, cols, rank_most, _ = left_ref.shape
    slot_most = near_ref.shape[0]
    lanes = cols * rank_most
    rank_at = lax.broadcasted_iota(jnp.int32, (rank_most, rows), 0)
    blocks = slab_blocks(slabs, width)
    for tile in range(tiles):
        x_ref[tile] = reorder_tile(tile, order_ref, blocks, part_ref[tile].astype(F32)).astype(BF16)
    meta_copy.wait()
    for tile in range(tiles):
        x = x_ref[tile]
        left = left_ref[tile].reshape(lanes, width)
        projected = lax.dot_general(left, x, (((1,), (1,)), ((), ())), preferred_element_type=F32)
        for col in range(cols):
            keep = rank_at < meta_ref[INDEX + 2 * slot_most + col * tiles + tile]
            kept = jnp.where(keep, projected[col * rank_most : (col + 1) * rank_most], 0.0)
            wide_ref[col, tile * rank_most : (tile + 1) * rank_most, :] = kept.astype(BF16)
    pieces = width // 128
    for col in range(cols):
        right = right_ref[:, col].reshape(tiles * rank_most, width)
        far = lax.dot_general(wide_ref[col], right, (((0,), (0,)), ((), ())), preferred_element_type=F32)
        for piece in range(pieces):
            sum_ref[col * pieces + piece] = far[:, piece * 128 : (piece + 1) * 128]
    for slot in range(slot_most):
        product = jnp.dot(x_ref[meta_ref[INDEX + slot]], near_ref[slot], preferred_element_type=F32)
        product = jnp.where(slot < meta_ref[COUNT], product, 0.0)
        at = meta_ref[INDEX + slot_most + slot] * pieces
        for piece in range(pieces):
            sum_ref[at + piece] += product[:, piece * 128 : (piece + 1) * 128]
    row = lax.axis_index("row")
    parts = out_ref.shape[1] // 128
    for part in range(parts):
        out_ref[:, part * 128 : (part + 1) * 128] = sum_ref[row * parts + part]
    for distance, send_ref in enumerate(send_refs, 1):
        to = jnp.bitwise_xor(row, distance)
        block = sum_ref[pl.ds(to * parts, parts)].reshape(parts * rows, 128)
        most = jnp.max(jnp.abs(block), axis=(0, 1), keepdims=True)
        power = jnp.ceil(jnp.log2(jnp.maximum(most, 1e-30)) - CODE_BITS)
        code = jnp.clip(jnp.round(block * jnp.exp2(-power)), -32767.0, 32767.0)
        send_ref[: parts * rows] = code.astype(jnp.int32).astype(jnp.int16)
        send_ref[parts * rows :] = jnp.broadcast_to(power.astype(jnp.int32), (16, 128)).astype(jnp.int16)


def finish_kernel(own_ref, *refs):
    *got_refs, out_ref, sum_ref, sems = refs
    rows = own_ref.shape[0]
    parts = own_ref.shape[1] // 128
    steps = [jnp.exp2(got_ref[parts * rows :].astype(F32)[:1]) for got_ref in got_refs]
    copies = []
    for part in range(parts):
        total = own_ref[:, part * 128 : (part + 1) * 128]
        for got_ref, step in zip(got_refs, steps):
            total = total + got_ref[part * rows : (part + 1) * rows].astype(F32) * step
        columns = slice(part * 128, (part + 1) * 128)
        sum_ref[:, columns] = total
        copies.append(pltpu.make_async_copy(sum_ref.at[:, columns], out_ref.at[:, columns], sems.at[part]))
        copies[-1].start()
    for copy in copies:
        copy.wait()


def local(sizes, adjoint, panel_order, left, right, tile_ranks, near_blocks, near_index, near_count):
    n_row, n_col = sizes
    rows, own_cols = adjoint.shape
    tiles, cols, rank_most, width = left.shape
    swap = lambda x, axis, n, d: lax.ppermute(x, axis, [(i, i ^ d) for i in range(n)])
    small = [near_count, near_index[0, 0], tile_ranks.T]
    scalars = sum(x.size for x in small)

    def reorder(slabs, distances, part=None, spare=0):
        slots = sum(slab.shape[0] * slab.shape[1] for slab in slabs)
        return pl.pallas_call(
            functools.partial(reorder_kernel, distances, part is None),
            out_shape=[jax.ShapeDtypeStruct((tiles, rows, width), BF16)]
            + ([jax.ShapeDtypeStruct((spare, own_cols), BF16), jax.ShapeDtypeStruct((-(-scalars // 128) * 128,), jnp.int32)] if spare else []),
            in_specs=[VMEM] * (1 + len(slabs) + (part is not None)) + [ANY] * (3 if part is None else 0),
            out_specs=[VMEM, VMEM, pl.BlockSpec(memory_space=pltpu.SMEM)] if spare else [VMEM],
            scratch_shapes=[pltpu.SMEM(x.shape, jnp.int32) for x in small] + [pltpu.SemaphoreType.DMA((3,))] if spare else [],
            cost_estimate=pl.CostEstimate(flops=2 * slots * tiles * width if part is None else 1000, bytes_accessed=0, transcendentals=0),
            compiler_params=pltpu.CompilerParams(vmem_limit_bytes=16 << 20),
            name="reorder",
        )(order, *slabs, *(small if part is None else [part]))

    if own_cols % width == 0 and own_cols & (own_cols - 1) == 0:
        order = jnp.bitwise_xor(panel_order, lax.axis_index("col") * own_cols).reshape(tiles, 1, width)
        far_off = [n_col - 2] + list(range(2, n_col - 2, 2))
        beside = swap(adjoint, "col", n_col, 1)
        near_part, got, meta = reorder([adjoint, beside], [[0], [1]], spare=len(far_off) * rows)
        for at, d in enumerate(far_off):
            got = lax.dynamic_update_slice_in_dim(got, swap(adjoint, "col", n_col, d), at * rows, 0)
        last, last_off = [swap(got, "col", n_col, 1)], [[d ^ 1 for d in far_off]]
        (part,) = reorder([got], [far_off], near_part)
    else:
        order = panel_order.reshape(tiles, 1, width)
        part = jnp.zeros((tiles, rows, width), BF16)
        meta = jnp.concatenate([x.reshape(-1) for x in small])
        meta = jnp.pad(meta, (0, -scalars % 128))
        last, last_off = [lax.all_gather(adjoint, "col", axis=1, tiled=True)], [[0]]
    out_cols = cols * width // n_row
    out, *sends = pl.pallas_call(
        functools.partial(main_kernel, last_off),
        out_shape=[jax.ShapeDtypeStruct((rows, out_cols), F32)]
        + [jax.ShapeDtypeStruct((rows * out_cols // 128 + 16, 128), jnp.int16)] * (n_row - 1),
        in_specs=[ANY] + [VMEM] * (5 + len(last)),
        out_specs=[VMEM] * n_row,
        scratch_shapes=[
            pltpu.VMEM((tiles, rows, width), BF16),
            pltpu.VMEM((cols, tiles * rank_most, rows), BF16),
            pltpu.VMEM((cols * width // 128, rows, 128), F32),
            pltpu.SMEM(meta.shape, jnp.int32),
            pltpu.SemaphoreType.DMA(()),
        ],
        compiler_params=pltpu.CompilerParams(vmem_limit_bytes=32 << 20),
        name="apply",
    )(meta, order, left, right, near_blocks[0, 0], part, *last)
    got = [swap(sends[d - 1], "row", n_row, d) for d in range(n_row - 1, 0, -1)]
    return pl.pallas_call(
        finish_kernel,
        out_shape=jax.ShapeDtypeStruct((rows, out_cols), F32),
        in_specs=[VMEM] * n_row,
        out_specs=ANY,
        scratch_shapes=[pltpu.VMEM((rows, out_cols), F32), pltpu.SemaphoreType.DMA((out_cols // 128,))],
        compiler_params=pltpu.CompilerParams(vmem_limit_bytes=4 << 20),
        name="finish",
    )(out, *got)


def solution(mesh):
    placed = (
        P(None, ("row", "col")),
        P("row", None),
        P("row", "col", None, None),
        P("row", "col", None, None),
        P("row", "col"),
        P("row", "col", None, None, None),
        P("row", "col", None, None),
        P("row", "col"),
    )
    sizes = (mesh.shape["row"], mesh.shape["col"])
    return jax.shard_map(
        functools.partial(local, sizes), mesh=mesh, in_specs=placed, out_specs=P(None, ("col", "row")), check_vma=False
    )
```
